256 devices in a mesh: expert: 64 (over z, x, core), mp: 4 (over y).
Axes of the slice: x: 4, y: 4, z: 8, core: 2. Of those that a mesh axis runs over, the one named last changes fastest.
Arguments:
- tokens: bfloat16 [64, 1024, 6144], P('expert', None, 'mp'), may hold values from -6 to 6
- cotangent: bfloat16 [64, 1024, 256], P('expert')
- counts: int32 [64], P('expert'), may hold values from 1 to 1024, as said below
- place_now: int32 [64], replicated, may hold values from 0 to 31, as said below
- partner: int32 [64], replicated, may hold values from 0 to 63, as said below
- place_next: int32 [64], replicated, may hold values from 0 to 31, as said below
- weight: float32 [64, 6144, 256], P('expert', 'mp'), as said below
- first_moment: float32 [64, 6144, 256], P('expert', 'mp'), as said below
- second_moment: float32 [64, 6144, 256], P('expert', 'mp'), as said below
Outputs:
- new_weight: float32 [64, 6144, 256], P('expert', 'mp')
- new_first: float32 [64, 6144, 256], P('expert', 'mp')
- new_second: float32 [64, 6144, 256], P('expert', 'mp')
The draws below stay inside these ranges and needn't reach their ends.
Inputs may be any that keep to these rules, and one draw needn't show every extreme that they name: `counts`: some slot has exactly 1024 live rows in every draw. `place_now`: every one of the 32 shards is held by exactly two slots. partner[s] is the other slot holding place_now[s]; partner[partner[s]] = s. `place_next`: every one of the 32 shards is held by exactly two slots. `weight`: slots holding the same shard in place_now have equal weights and moments. `first_moment`: slots holding the same shard in place_now have equal weights and moments. `second_moment`: Positive; slots holding the same shard in place_now have equal values.
All inputs are finite; a program needn't handle non-finite values.
Results may differ from the reference program's by a relative error of at most 0.0003.
Values sent between devices are 32-bit elements; how exact they have to be, the bound alone decides.
No kernel may reach another device: no remote copies, remote signals or barrier semaphores. Data moves between devices by JAX's collectives and lax.ppermute only.
A program may use at most 64 MiB of HBM per device.

```python
import math
import jax
import jax.numpy as jnp
from jax import lax

D = 6144
HS = 256
ROWS = 1024
SLOTS = 64
UNITS = 32


def placements(key):
    base = jax.random.fold_in(key, 101)
    key_one, key_two = jax.random.split(base, 2)
    perm = jax.random.permutation(key_one, SLOTS).astype(jnp.int32)
    current = perm % UNITS
    order = jnp.argsort(current, stable=True).astype(jnp.int32)
    first = order[0::2]
    second = order[1::2]
    pairing = jnp.zeros((SLOTS,), jnp.int32).at[first].set(second).at[second].set(first)
    chosen = jax.random.permutation(key_two, SLOTS).astype(jnp.int32)[:max(2, SLOTS // 4)]
    upcoming = current.at[chosen].set(current[jnp.roll(chosen, 1)])
    return (current, pairing, upcoming)


def unit_table(key, salt, kind):
    key = jax.random.fold_in(key, salt)
    current = placements(key)[0]
    if kind == 2:
        table = jnp.exp(jax.random.uniform(key, (UNITS, D, HS), jnp.float32, -0.7, 0.7))
    else:
        table = jax.random.normal(key, (UNITS, D, HS), jnp.float32) * 0.5
    return table[current]


def draw_place_now(key, part):
    return placements(key)[0]


def draw_partner(key, part):
    return placements(key)[1]


def draw_place_next(key, part):
    return placements(key)[2]


def draw_counts(key, part):
    key = jax.random.fold_in(key, 7)
    key_one, key_two = jax.random.split(key, 2)
    base = jax.random.randint(key_one, (SLOTS,), 0, ROWS, jnp.int32)
    live = 1 + base * base // ROWS
    pick = jax.random.randint(key_two, (), 0, SLOTS, jnp.int32)
    return live.at[pick].set(ROWS)


def draw_cotangent(key, part):
    key = jax.random.fold_in(key, 13)
    key_one = jax.random.fold_in(key, 0)
    rising = 1.0 + 2.0 * jnp.arange(SLOTS, dtype=jnp.float32) / max(SLOTS - 1, 1)
    values = jax.random.normal(key_one, (SLOTS, ROWS, HS), jnp.float32)
    return (values * rising[:, None, None]).astype(jnp.bfloat16)


def draw_weight(key, part):
    return unit_table(key, 21, 0)


def draw_first_moment(key, part):
    return unit_table(key, 22, 1)


def draw_second_moment(key, part):
    return unit_table(key, 23, 2)


def level_of(stream_key, extent, cuts, smallest, largest):
    factor_of, own = 1.0, jax.random.fold_in(stream_key, 6)
    for dim, shards_of in cuts:
        draws = jnp.exp(jax.random.uniform(jax.random.fold_in(own, dim), (shards_of,), jnp.float32, smallest / len(cuts), largest / len(cuts)))
        factor_of = factor_of * jnp.repeat(draws, extent[dim] // shards_of).reshape([-1 if axis == dim else 1 for axis in range(len(extent))])
    return factor_of


def noise(stream_key, dims, scale, most, cuts=(), held_as=jnp.bfloat16):
    gain = level_of(stream_key, dims, cuts, -0.22, 0.18) if cuts else 1.0
    values = jax.random.normal(stream_key, dims, jnp.float32) * scale * gain
    return jnp.minimum(jnp.maximum(values, -most), most).astype(held_as)


def setup_inputs(seed: int = 0) -> dict:
    splits = jax.random.split(jax.random.key(seed), 10)
    return {
        "tokens": noise(splits[0], (SLOTS, ROWS, D), 1.0, 6.0, ((0, 64), (2, 4))),
        "cotangent": draw_cotangent(jax.random.fold_in(splits[9], 71), 0),
        "counts": draw_counts(jax.random.fold_in(splits[9], 71), 0),
        "place_now": draw_place_now(jax.random.fold_in(splits[9], 71), 0),
        "partner": draw_partner(jax.random.fold_in(splits[9], 71), 0),
        "place_next": draw_place_next(jax.random.fold_in(splits[9], 71), 0),
        "weight": draw_weight(jax.random.fold_in(splits[9], 71), 0),
        "first_moment": draw_first_moment(jax.random.fold_in(splits[9], 71), 0),
        "second_moment": draw_second_moment(jax.random.fold_in(splits[9], 71), 0),
    }


def reference(tokens, cotangent, counts, place_now, partner, place_next, weight, first_moment, second_moment):
    row_ids = jnp.arange(ROWS, dtype=jnp.int32)

    def slot_grad(items):
        block, grad_rows, live = items
        masked = jnp.where((row_ids < live)[:, None], grad_rows, jnp.zeros_like(grad_rows))
        return jnp.dot(block.T, masked, preferred_element_type=jnp.float32)
    grads = lax.map(slot_grad, (tokens, cotangent, counts))
    raw = grads + grads[partner]
    sumsq = 0.5 * jnp.sum(raw * raw)
    limit = 4.0 * math.sqrt(UNITS * D * HS)
    clip = jnp.minimum(jnp.float32(1.0), limit / jnp.sqrt(sumsq + 1e-06))
    total = clip * raw
    first_new = 0.9 * first_moment + 0.1 * total
    second_new = 0.95 * second_moment + 0.05 * total * total
    step_size = first_new / (1.0 - 0.9 ** 10) / (jnp.sqrt(second_new / (1.0 - 0.95 ** 10)) + 1e-08)
    updated = weight - 0.1 * (step_size + 0.3 * weight)
    equal = place_now[None, :] == place_next[:, None]
    lowest = jnp.argmax(equal, axis=1).astype(jnp.int32)
    source = jnp.where(place_now == place_next, jnp.arange(SLOTS, dtype=jnp.int32), lowest)
    return (updated[source], first_new[source], second_new[source])
```

```python
import functools
import math

import jax
import jax.numpy as jnp
from jax import lax
from jax.experimental import pallas as pl
from jax.experimental.pallas import tpu as pltpu
from jax.sharding import PartitionSpec as P

LANES = 128


def local_grad(block, grad_rows, live):
    rows_total = block.shape[0]
    row_ids = jnp.arange(rows_total, dtype=jnp.int32)
    masked = jnp.where((row_ids < live)[:, None], grad_rows, jnp.zeros_like(grad_rows))
    return jnp.einsum("rd,rh->dh", block, masked, preferred_element_type=jnp.float32)


def sumsq_kernel(slots, partner_ref, grad_ref, out_ref):
    def body(slot, acc):
        raw = grad_ref[slot] + grad_ref[partner_ref[slot]]
        return acc + raw * raw

    zero = jnp.zeros(grad_ref.shape[1:], jnp.float32)
    acc = lax.fori_loop(0, slots, body, zero, unroll=4)
    rows, cols = acc.shape
    part = sum(
        acc[r : r + 8, c : c + LANES] for r in range(0, rows, 8) for c in range(0, cols, LANES)
    )
    out_ref[...] = jnp.broadcast_to(0.5 * jnp.sum(part), out_ref.shape)


def update_kernel(
    slots, limit, source_ref, partner_ref, sum_ref, grad_ref, state_ref, out_ref
):
    clip = jnp.minimum(jnp.float32(1.0), limit / jnp.sqrt(sum_ref[...] + 1e-06))

    def update(slot, carry):
        source = source_ref[slot]
        other = partner_ref[source]
        for start in range(0, grad_ref.shape[2], LANES):
            cols = pl.ds(start, LANES)
            total = clip * (grad_ref[source, :, cols] + grad_ref[other, :, cols])
            weight = state_ref[source, 0, :, cols]
            first = 0.9 * state_ref[source, 1, :, cols] + 0.1 * total
            second = 0.95 * state_ref[source, 2, :, cols] + 0.05 * total * total
            step = (first / (1.0 - 0.9**10)) / (jnp.sqrt(second / (1.0 - 0.95**10)) + 1e-08)
            out_ref[slot, 0, :, cols] = weight - 0.1 * (step + 0.3 * weight)
            out_ref[slot, 1, :, cols] = first
            out_ref[slot, 2, :, cols] = second
        return carry

    lax.fori_loop(0, slots, update, 0, unroll=4)


def shifted(value, axis, pairs_of):
    total = value
    for pairs in pairs_of:
        total = total + lax.ppermute(value, axis, pairs)
    return total


def all_sum(value):
    slots = lax.axis_size("expert")
    width = lax.axis_size("mp")
    inner = 8
    outer = slots // inner
    value = shifted(
        value, "mp", [[(i, (i + k) % width) for i in range(width)] for k in range(1, width)]
    )
    value = shifted(
        value, "expert", [[(i, i ^ k) for i in range(slots)] for k in range(1, inner)]
    )
    return shifted(
        value,
        "expert",
        [[(i, (i + k * inner) % slots) for i in range(slots)] for k in range(1, outer)],
    )


def on_device(
    tokens, cotangent, counts, place_now, partner, place_next, weight, first_moment, second_moment
):
    slots = lax.axis_size("expert")
    units = slots // 2
    width_dev = weight.shape[1]
    hidden = weight.shape[2]
    rows = width_dev // slots
    limit = 4.0 * math.sqrt(units * width_dev * lax.axis_size("mp") * hidden)

    equal = place_now[None, :] == place_next[:, None]
    lowest = jnp.argmax(equal, axis=1).astype(jnp.int32)
    source = jnp.where(place_now == place_next, jnp.arange(slots, dtype=jnp.int32), lowest)

    grads = local_grad(tokens[0], cotangent[0], counts[0]).reshape(slots, rows, hidden)
    states = jnp.stack(
        [array.reshape(slots, rows, hidden) for array in (weight, first_moment, second_moment)],
        axis=1,
    )
    spread = lax.all_to_all(grads, "expert", split_axis=0, concat_axis=0, tiled=True)
    spread, states = lax.optimization_barrier((spread, states))
    states = lax.all_to_all(states, "expert", split_axis=0, concat_axis=0, tiled=True)

    smem = pl.BlockSpec(memory_space=pltpu.SMEM)
    part = pl.pallas_call(
        functools.partial(sumsq_kernel, slots),
        out_shape=jax.ShapeDtypeStruct((8, LANES), jnp.float32),
        in_specs=[smem, pl.BlockSpec(memory_space=pltpu.VMEM)],
        out_specs=pl.BlockSpec(memory_space=pltpu.VMEM),
        cost_estimate=pl.CostEstimate(
            flops=spread.size, bytes_accessed=spread.size * 4, transcendentals=0
        ),
    )(partner, spread)
    sumsq = all_sum(part)

    chunk = 8
    out = pl.pallas_call(
        functools.partial(update_kernel, slots, limit),
        grid=(rows // chunk,),
        out_shape=jax.ShapeDtypeStruct((slots, 3, rows, hidden), jnp.float32),
        in_specs=[
            smem,
            smem,
            pl.BlockSpec((8, LANES), lambda i: (0, 0)),
            pl.BlockSpec((slots, chunk, hidden), lambda i: (0, i, 0)),
            pl.BlockSpec((slots, 3, chunk, hidden), lambda i: (0, 0, i, 0)),
        ],
        out_specs=pl.BlockSpec((slots, 3, chunk, hidden), lambda i: (0, 0, i, 0)),
        compiler_params=pltpu.CompilerParams(vmem_limit_bytes=32 * 2**20),
    )(source, partner, sumsq, spread, states)
    out = lax.all_to_all(out, "expert", split_axis=0, concat_axis=0, tiled=True)
    return tuple(out[:, k].reshape(weight.shape) for k in range(3))


def solution(mesh):
    placed = (
        P("expert", None, "mp"),
        P("expert", None, None),
        P("expert"),
        P(),
        P(),
        P(),
        P("expert", "mp", None),
        P("expert", "mp", None),
        P("expert", "mp", None),
    )
    return jax.shard_map(
        on_device,
        mesh=mesh,
        in_specs=placed,
        out_specs=(P("expert", "mp", None), P("expert", "mp", None), P("expert", "mp", None)),
        check_vma=False,
    )
```

```python
import functools
import math

import jax
import jax.numpy as jnp
from jax import lax
from jax.experimental import pallas as pl
from jax.experimental.pallas import tpu as pltpu
from jax.sharding import PartitionSpec as P

LANES = 128


def local_grad(block, grad_rows, live):
    rows_total = block.shape[0]
    row_ids = jnp.arange(rows_total, dtype=jnp.int32)
    masked = jnp.where((row_ids < live)[:, None], grad_rows, jnp.zeros_like(grad_rows))
    return jnp.einsum("rd,rh->dh", block, masked, preferred_element_type=jnp.float32)


def sumsq_kernel(slots, partner_ref, grad_ref, out_ref):
    def body(slot, acc):
        raw = grad_ref[slot] + grad_ref[partner_ref[slot]]
        return acc + raw * raw

    zero = jnp.zeros(grad_ref.shape[1:], jnp.float32)
    acc = lax.fori_loop(0, slots, body, zero, unroll=4)
    rows, cols = acc.shape
    part = sum(
        acc[r : r + 8, c : c + LANES] for r in range(0, rows, 8) for c in range(0, cols, LANES)
    )
    out_ref[...] = jnp.broadcast_to(0.5 * jnp.sum(part), out_ref.shape)


def update_kernel(
    slots,
    limit,
    source_ref,
    partner_ref,
    sum_ref,
    grad_ref,
    weight_ref,
    first_ref,
    second_ref,
    out_ref,
):
    clip = jnp.minimum(jnp.float32(1.0), limit / jnp.sqrt(sum_ref[...] + 1e-06))

    def update(slot, carry):
        source = source_ref[slot]
        other = partner_ref[source]
        for start in range(0, grad_ref.shape[2], LANES):
            cols = pl.ds(start, LANES)
            total = clip * (grad_ref[source, :, cols] + grad_ref[other, :, cols])
            weight = weight_ref[source, :, cols]
            first = 0.9 * first_ref[source, :, cols] + 0.1 * total
            second = 0.95 * second_ref[source, :, cols] + 0.05 * total * total
            root = jnp.sqrt(second * (1.0 / (1.0 - 0.95**10))) + 1e-08
            step = (first * (1.0 / (1.0 - 0.9**10))) / root
            out_ref[slot, 0, :, cols] = weight - 0.1 * (step + 0.3 * weight)
            out_ref[slot, 1, :, cols] = first
            out_ref[slot, 2, :, cols] = second
        return carry

    lax.fori_loop(0, slots, update, 0, unroll=8)


def shifted(value, axis, pairs_of):
    total = value
    for pairs in pairs_of:
        total = total + lax.ppermute(value, axis, pairs)
    return total


def plane_sum(value, slots, inner):
    value = shifted(value, "expert", [[(i, i ^ 1) for i in range(slots)]])
    return shifted(
        value,
        "expert",
        [
            [(i, i // inner * inner + (i + k) % inner) for i in range(slots)]
            for k in range(2, inner, 2)
        ],
    )


def all_sum(value):
    slots = lax.axis_size("expert")
    width = lax.axis_size("mp")
    inner = 8
    value = shifted(
        value, "mp", [[(i, (i + k) % width) for i in range(width)] for k in range(1, width)]
    )
    value = plane_sum(value, slots, inner)
    spots = [(i, (i + i % inner * inner) % slots) for i in range(slots) if i % inner]
    moved = lax.ppermute(value, "expert", spots)
    value = jnp.where(lax.axis_index("expert") % inner == 0, value, moved)
    return plane_sum(value, slots, inner)


def to_pieces(array):
    return lax.all_to_all(array, "expert", split_axis=0, concat_axis=0, tiled=True)


def on_device(
    tokens, cotangent, counts, place_now, partner, place_next, weight, first_moment, second_moment
):
    slots = lax.axis_size("expert")
    units = slots // 2
    width_dev = weight.shape[1]
    hidden = weight.shape[2]
    rows = width_dev // slots
    limit = 4.0 * math.sqrt(units * width_dev * lax.axis_size("mp") * hidden)

    equal = place_now[None, :] == place_next[:, None]
    lowest = jnp.argmax(equal, axis=1).astype(jnp.int32)
    source = jnp.where(place_now == place_next, jnp.arange(slots, dtype=jnp.int32), lowest)

    weight_rows = weight.reshape(slots, rows, hidden)
    first_rows = first_moment.reshape(slots, rows, hidden)
    second_rows = second_moment.reshape(slots, rows, hidden)
    weight_rows = to_pieces(weight_rows)
    grads = local_grad(tokens[0], cotangent[0], counts[0]).reshape(slots, rows, hidden)
    weight_rows, grads = lax.optimization_barrier((weight_rows, grads))
    spread = to_pieces(grads)
    spread, first_rows = lax.optimization_barrier((spread, first_rows))
    first_rows = to_pieces(first_rows)
    first_rows, second_rows = lax.optimization_barrier((first_rows, second_rows))
    second_rows = to_pieces(second_rows)

    smem = pl.BlockSpec(memory_space=pltpu.SMEM)
    part = pl.pallas_call(
        functools.partial(sumsq_kernel, slots),
        out_shape=jax.ShapeDtypeStruct((8, LANES), jnp.float32),
        in_specs=[smem, pl.BlockSpec(memory_space=pltpu.VMEM)],
        out_specs=pl.BlockSpec(memory_space=pltpu.VMEM),
        cost_estimate=pl.CostEstimate(
            flops=spread.size, bytes_accessed=spread.size * 4, transcendentals=0
        ),
    )(partner, spread)
    sumsq = all_sum(part)

    chunk = 8
    out = pl.pallas_call(
        functools.partial(update_kernel, slots, limit),
        grid=(rows // chunk,),
        out_shape=jax.ShapeDtypeStruct((slots, 3, rows, hidden), jnp.float32),
        in_specs=[
            smem,
            smem,
            pl.BlockSpec((8, LANES), lambda i: (0, 0)),
            pl.BlockSpec((slots, chunk, hidden), lambda i: (0, i, 0)),
            pl.BlockSpec((slots, chunk, hidden), lambda i: (0, i, 0)),
            pl.BlockSpec((slots, chunk, hidden), lambda i: (0, i, 0)),
            pl.BlockSpec((slots, chunk, hidden), lambda i: (0, i, 0)),
        ],
        out_specs=pl.BlockSpec((slots, 3, chunk, hidden), lambda i: (0, 0, i, 0)),
        compiler_params=pltpu.CompilerParams(vmem_limit_bytes=32 * 2**20),
    )(source, partner, sumsq, spread, weight_rows, first_rows, second_rows)
    out = to_pieces(out)
    return tuple(out[:, k].reshape(weight.shape) for k in range(3))


def solution(mesh):
    placed = (
        P("expert", None, "mp"),
        P("expert", None, None),
        P("expert"),
        P(),
        P(),
        P(),
        P("expert", "mp", None),
        P("expert", "mp", None),
        P("expert", "mp", None),
    )
    return jax.shard_map(
        on_device,
        mesh=mesh,
        in_specs=placed,
        out_specs=(P("expert", "mp", None), P("expert", "mp", None), P("expert", "mp", None)),
        check_vma=False,
    )
```

```python
import functools
import math

import jax
import jax.numpy as jnp
from jax import lax
from jax.experimental import pallas as pl
from jax.experimental.pallas import tpu as pltpu
from jax.sharding import PartitionSpec as P

LANES = 128
INNER = 8


def grad_kernel(live_ref, block_ref, rows_ref, out_ref):
    rows = rows_ref[...].astype(jnp.float32)
    row_ids = lax.broadcasted_iota(jnp.int32, rows.shape, 0)
    masked = jnp.where(row_ids < live_ref[0], rows, jnp.zeros_like(rows)).astype(jnp.bfloat16)
    out_ref[...] = lax.dot_general(
        block_ref[...], masked, (((0,), (0,)), ((), ())), preferred_element_type=jnp.float32
    )


def local_grad(block, grad_rows, live):
    rows, width = block.shape
    hidden = grad_rows.shape[1]
    tile = width // 2
    return pl.pallas_call(
        grad_kernel,
        grid=(width // tile,),
        out_shape=jax.ShapeDtypeStruct((width, hidden), jnp.float32),
        in_specs=[
            pl.BlockSpec(memory_space=pltpu.SMEM),
            pl.BlockSpec((rows, tile), lambda i: (0, i)),
            pl.BlockSpec((rows, hidden), lambda i: (0, 0)),
        ],
        out_specs=pl.BlockSpec((tile, hidden), lambda i: (i, 0)),
        compiler_params=pltpu.CompilerParams(vmem_limit_bytes=56 * 2**20),
        cost_estimate=pl.CostEstimate(
            flops=2 * rows * width * hidden,
            bytes_accessed=2 * rows * (width + hidden) + 4 * width * hidden,
            transcendentals=0,
        ),
    )(live, block, grad_rows)


def sumsq_kernel(slots, partner_ref, grad_ref, out_ref):
    def body(slot, acc):
        raw = grad_ref[slot] + grad_ref[partner_ref[slot]]
        return acc + raw * raw

    zero = jnp.zeros(grad_ref.shape[1:], jnp.float32)
    acc = lax.fori_loop(0, slots, body, zero, unroll=4)
    rows, cols = acc.shape
    part = sum(
        acc[r : r + 8, c : c + LANES] for r in range(0, rows, 8) for c in range(0, cols, LANES)
    )
    out_ref[...] = jnp.broadcast_to(0.5 * jnp.sum(part), out_ref.shape)


def update_kernel(
    slots,
    limit,
    source_ref,
    partner_ref,
    sum_ref,
    grad_ref,
    state_ref,
    out_ref,
):
    clip = jnp.minimum(jnp.float32(1.0), limit / jnp.sqrt(sum_ref[0:1, 0:1] + 1e-06))
    clip = jnp.broadcast_to(clip, (8, grad_ref.shape[2]))

    def update(slot, carry):
        source = source_ref[slot]
        other = partner_ref[source]
        for top in range(0, grad_ref.shape[1], 8):
            rows = pl.ds(top, 8)
            total = clip * (grad_ref[source, rows] + grad_ref[other, rows])
            weight = state_ref[source, 0, rows]
            first = 0.9 * state_ref[source, 1, rows] + 0.1 * total
            second = 0.95 * state_ref[source, 2, rows] + 0.05 * total * total
            root = jnp.sqrt(second * (1.0 / (1.0 - 0.95**10))) + 1e-08
            step = (first * (1.0 / (1.0 - 0.9**10))) / root
            out_ref[slot, 0, rows] = weight - 0.1 * (step + 0.3 * weight)
            out_ref[slot, 1, rows] = first
            out_ref[slot, 2, rows] = second
        return carry

    lax.fori_loop(0, slots, update, 0, unroll=4)


def shifted(value, axis, pairs_of):
    total = value
    for pairs in pairs_of:
        total = total + lax.ppermute(value, axis, pairs)
    return total


def plane_sum(value, slots, inner):
    value = shifted(value, "expert", [[(i, i ^ 1) for i in range(slots)]])
    return shifted(
        value,
        "expert",
        [
            [(i, i // inner * inner + (i + k) % inner) for i in range(slots)]
            for k in range(2, inner, 2)
        ],
    )


def all_sum(value):
    slots = lax.axis_size("expert")
    width = lax.axis_size("mp")
    value = shifted(
        value, "mp", [[(i, (i + k) % width) for i in range(width)] for k in range(1, width)]
    )
    value = plane_sum(value, slots, INNER)
    half = slots // INNER // 2
    core = lax.axis_index("expert") % 2
    total = jnp.where(core == 0, value, jnp.zeros_like(value))
    for k in range(half):
        spots = [
            (i, (i + (k + i % 2 * half) * INNER) % slots) for i in range(slots) if k + i % 2
        ]
        total = total + lax.ppermute(value, "expert", spots)
    return shifted(total, "expert", [[(i, i ^ 1) for i in range(slots)]])


def to_pieces(array):
    return lax.all_to_all(array, "expert", split_axis=0, concat_axis=0, tiled=True)


def on_device(
    tokens, cotangent, counts, place_now, partner, place_next, weight, first_moment, second_moment
):
    slots = lax.axis_size("expert")
    units = slots // 2
    width_dev = weight.shape[1]
    hidden = weight.shape[2]
    rows = width_dev // slots
    limit = 4.0 * math.sqrt(units * width_dev * lax.axis_size("mp") * hidden)

    pair = jnp.clip(partner, 0, slots - 1)
    equal = place_now[None, :] == place_next[:, None]
    lowest = jnp.argmax(equal, axis=1).astype(jnp.int32)
    source = jnp.where(place_now == place_next, jnp.arange(slots, dtype=jnp.int32), lowest)

    grads = local_grad(tokens[0], cotangent[0], counts).reshape(slots, rows, hidden)
    states = jnp.stack(
        [array.reshape(slots, rows, hidden) for array in (weight, first_moment, second_moment)],
        axis=1,
    )
    spread = to_pieces(grads)
    spread, states = lax.optimization_barrier((spread, states))
    states = to_pieces(states)

    smem = pl.BlockSpec(memory_space=pltpu.SMEM)
    part = pl.pallas_call(
        functools.partial(sumsq_kernel, slots),
        out_shape=jax.ShapeDtypeStruct((8, LANES), jnp.float32),
        in_specs=[smem, pl.BlockSpec(memory_space=pltpu.VMEM)],
        out_specs=pl.BlockSpec(memory_space=pltpu.VMEM),
        cost_estimate=pl.CostEstimate(
            flops=spread.size, bytes_accessed=spread.size * 4, transcendentals=0
        ),
    )(pair, spread)
    sumsq = all_sum(part)

    vmem = pl.BlockSpec(memory_space=pltpu.VMEM)
    out = pl.pallas_call(
        functools.partial(update_kernel, slots, limit),
        out_shape=jax.ShapeDtypeStruct((slots, 3, rows, hidden), jnp.float32),
        in_specs=[smem, smem, vmem, vmem, vmem],
        out_specs=vmem,
        compiler_params=pltpu.CompilerParams(vmem_limit_bytes=32 * 2**20),
    )(source, pair, sumsq, spread, states)
    out = to_pieces(out)
    return tuple(out[:, k].reshape(weight.shape) for k in range(3))


def solution(mesh):
    placed = (
        P("expert", None, "mp"),
        P("expert", None, None),
        P("expert"),
        P(),
        P(),
        P(),
        P("expert", "mp", None),
        P("expert", "mp", None),
        P("expert", "mp", None),
    )
    return jax.shard_map(
        on_device,
        mesh=mesh,
        in_specs=placed,
        out_specs=(P("expert", "mp", None), P("expert", "mp", None), P("expert", "mp", None)),
        check_vma=False,
    )
```

```python
import functools
import math

import jax
import jax.numpy as jnp
from jax import lax
from jax.experimental import pallas as pl
from jax.experimental.pallas import tpu as pltpu
from jax.sharding import PartitionSpec as P

LANES = 128
INNER = 8


def grad_kernel(live_ref, block_ref, rows_ref, out_ref):
    rows = rows_ref[...].astype(jnp.float32)
    row_ids = lax.broadcasted_iota(jnp.int32, rows.shape, 0)
    masked = jnp.where(row_ids < live_ref[0], rows, jnp.zeros_like(rows)).astype(jnp.bfloat16)
    out_ref[...] = lax.dot_general(
        block_ref[...], masked, (((0,), (0,)), ((), ())), preferred_element_type=jnp.float32
    )


def local_grad(block, grad_rows, live):
    rows, width = block.shape
    hidden = grad_rows.shape[1]
    tile = width // 2
    return pl.pallas_call(
        grad_kernel,
        grid=(width // tile,),
        out_shape=jax.ShapeDtypeStruct((width, hidden), jnp.float32),
        in_specs=[
            pl.BlockSpec(memory_space=pltpu.SMEM),
            pl.BlockSpec((rows, tile), lambda i: (0, i)),
            pl.BlockSpec((rows, hidden), lambda i: (0, 0)),
        ],
        out_specs=pl.BlockSpec((tile, hidden), lambda i: (i, 0)),
        compiler_params=pltpu.CompilerParams(vmem_limit_bytes=56 * 2**20),
        cost_estimate=pl.CostEstimate(
            flops=2 * rows * width * hidden,
            bytes_accessed=2 * rows * (width + hidden) + 4 * width * hidden,
            transcendentals=0,
        ),
    )(live, block, grad_rows)


def sumsq_kernel(slots, partner_ref, grad_ref, out_ref):
    def body(slot, acc):
        raw = grad_ref[slot] + grad_ref[partner_ref[slot]]
        return acc + raw * raw

    zero = jnp.zeros(grad_ref.shape[1:], jnp.float32)
    acc = lax.fori_loop(0, slots, body, zero, unroll=4)
    rows, cols = acc.shape
    part = sum(
        acc[r : r + 8, c : c + LANES] for r in range(0, rows, 8) for c in range(0, cols, LANES)
    )
    out_ref[...] = jnp.broadcast_to(0.5 * jnp.sum(part), out_ref.shape)


def update_kernel(
    slots,
    limit,
    source_ref,
    partner_ref,
    sum_ref,
    grad_ref,
    state_ref,
    out_ref,
):
    clip = jnp.minimum(jnp.float32(1.0), limit / jnp.sqrt(sum_ref[0:1, 0:1] + 1e-06))
    clip = jnp.broadcast_to(clip, (8, grad_ref.shape[2]))

    def update(slot, carry):
        source = source_ref[slot]
        other = partner_ref[source]
        for top in range(0, grad_ref.shape[1], 8):
            rows = pl.ds(top, 8)
            total = clip * (grad_ref[source, rows] + grad_ref[other, rows])
            weight = state_ref[source, 0, rows]
            first = 0.9 * state_ref[source, 1, rows] + 0.1 * total
            second = 0.95 * state_ref[source, 2, rows] + 0.05 * total * total
            root = jnp.sqrt(second * (1.0 / (1.0 - 0.95**10))) + 1e-08
            step = (first * (1.0 / (1.0 - 0.9**10))) / root
            out_ref[slot, 0, rows] = weight - 0.1 * (step + 0.3 * weight)
            out_ref[slot, 1, rows] = first
            out_ref[slot, 2, rows] = second
        return carry

    lax.fori_loop(0, slots, update, 0, unroll=4)


def shifted(value, axis, pairs_of):
    total = value
    for pairs in pairs_of:
        total = total + lax.ppermute(value, axis, pairs)
    return total


def plane_sum(value, slots, inner):
    value = shifted(value, "expert", [[(i, i ^ 1) for i in range(slots)]])
    return shifted(
        value,
        "expert",
        [
            [(i, i // inner * inner + (i + k) % inner) for i in range(slots)]
            for k in range(2, inner, 2)
        ],
    )


def all_sum(value):
    slots = lax.axis_size("expert")
    width = lax.axis_size("mp")
    value = shifted(
        value, "mp", [[(i, (i + k) % width) for i in range(width)] for k in range(1, width)]
    )
    value = plane_sum(value, slots, INNER)
    half = slots // INNER // 2
    core = lax.axis_index("expert") % 2
    total = jnp.where(core == 0, value, jnp.zeros_like(value))
    for k in range(half):
        spots = [
            (i, (i + (k + i % 2 * half) * INNER) % slots) for i in range(slots) if k + i % 2
        ]
        total = total + lax.ppermute(value, "expert", spots)
    return shifted(total, "expert", [[(i, i ^ 1) for i in range(slots)]])


def to_pieces(array):
    return lax.all_to_all(array, "expert", split_axis=0, concat_axis=0, tiled=True)


def on_device(
    tokens, cotangent, counts, place_now, partner, place_next, weight, first_moment, second_moment
):
    slots = lax.axis_size("expert")
    units = slots // 2
    width_dev = weight.shape[1]
    hidden = weight.shape[2]
    rows = width_dev // slots
    limit = 4.0 * math.sqrt(units * width_dev * lax.axis_size("mp") * hidden)

    pair = jnp.clip(partner, 0, slots - 1)
    equal = place_now[None, :] == place_next[:, None]
    lowest = jnp.argmax(equal, axis=1).astype(jnp.int32)
    source = jnp.where(place_now == place_next, jnp.arange(slots, dtype=jnp.int32), lowest)

    grads = local_grad(tokens[0], cotangent[0], counts).reshape(slots, rows, hidden)
    states = jnp.stack(
        [array.reshape(slots, rows, hidden) for array in (weight, first_moment, second_moment)],
        axis=1,
    )
    spread = to_pieces(grads)
    spread, states = lax.optimization_barrier((spread, states))
    states = to_pieces(states)

    smem = pl.BlockSpec(memory_space=pltpu.SMEM)
    part = pl.pallas_call(
        functools.partial(sumsq_kernel, slots),
        out_shape=jax.ShapeDtypeStruct((8, LANES), jnp.float32),
        in_specs=[smem, pl.BlockSpec(memory_space=pltpu.VMEM)],
        out_specs=pl.BlockSpec(memory_space=pltpu.VMEM),
        compiler_params=pltpu.CompilerParams(vmem_limit_bytes=8 * 2**20),
        cost_estimate=pl.CostEstimate(
            flops=spread.size, bytes_accessed=spread.size * 4, transcendentals=0
        ),
    )(pair, spread)
    sumsq = all_sum(part)

    vmem = pl.BlockSpec(memory_space=pltpu.VMEM)
    out = pl.pallas_call(
        functools.partial(update_kernel, slots, limit),
        out_shape=jax.ShapeDtypeStruct((slots, 3, rows, hidden), jnp.float32),
        in_specs=[smem, smem, vmem, vmem, vmem],
        out_specs=vmem,
        compiler_params=pltpu.CompilerParams(vmem_limit_bytes=16 * 2**20),
    )(source, pair, sumsq, spread, states)
    out = to_pieces(out)
    return tuple(out[:, k].reshape(weight.shape) for k in range(3))


def solution(mesh):
    placed = (
        P("expert", None, "mp"),
        P("expert", None, None),
        P("expert"),
        P(),
        P(),
        P(),
        P("expert", "mp", None),
        P("expert", "mp", None),
        P("expert", "mp", None),
    )
    return jax.shard_map(
        on_device,
        mesh=mesh,
        in_specs=placed,
        out_specs=(P("expert", "mp", None), P("expert", "mp", None), P("expert", "mp", None)),
        check_vma=False,
    )
```

```python
import functools
import math

import jax
import jax.numpy as jnp
from jax import lax
from jax.experimental import pallas as pl
from jax.experimental.pallas import tpu as pltpu
from jax.sharding import PartitionSpec as P

LANES = 128
INNER = 8
ROUNDS = (4, 4)


def grad_kernel(live_ref, block_ref, rows_ref, weight_ref, out_ref):
    rows = rows_ref[...].astype(jnp.float32)
    row_ids = lax.broadcasted_iota(jnp.int32, rows.shape, 0)
    masked = jnp.where(row_ids < live_ref[0], rows, jnp.zeros_like(rows)).astype(jnp.bfloat16)
    grads = lax.dot_general(
        block_ref[...], masked, (((0,), (0,)), ((), ())), preferred_element_type=jnp.float32
    )
    out_ref[:, 0] = grads.reshape(weight_ref.shape)
    out_ref[:, 1] = weight_ref[...]


def grad_and_weight(block, grad_rows, live, weight):
    rows, width = block.shape
    pieces, piece_rows, hidden = weight.shape
    steps = 2
    tile, group = width // steps, pieces // steps
    return pl.pallas_call(
        grad_kernel,
        grid=(steps,),
        out_shape=jax.ShapeDtypeStruct((pieces, 2, piece_rows, hidden), jnp.float32),
        in_specs=[
            pl.BlockSpec(memory_space=pltpu.SMEM),
            pl.BlockSpec((rows, tile), lambda i: (0, i)),
            pl.BlockSpec((rows, hidden), lambda i: (0, 0)),
            pl.BlockSpec((group, piece_rows, hidden), lambda i: (i, 0, 0)),
        ],
        out_specs=pl.BlockSpec((group, 2, piece_rows, hidden), lambda i: (i, 0, 0, 0)),
        compiler_params=pltpu.CompilerParams(vmem_limit_bytes=56 * 2**20),
        cost_estimate=pl.CostEstimate(
            flops=2 * rows * width * hidden,
            bytes_accessed=2 * rows * (width + hidden) + 12 * width * hidden,
            transcendentals=0,
        ),
    )(live, block, grad_rows, weight)


def sumsq_kernel(slots, partner_ref, grad_ref, out_ref):
    def body(slot, acc):
        raw = grad_ref[slot, 0] + grad_ref[partner_ref[slot], 0]
        return acc + raw * raw

    zero = jnp.zeros(grad_ref.shape[2:], jnp.float32)
    acc = lax.fori_loop(0, slots, body, zero, unroll=4)
    rows, cols = acc.shape
    part = sum(
        acc[r : r + 8, c : c + LANES] for r in range(0, rows, 8) for c in range(0, cols, LANES)
    )
    out_ref[...] = jnp.broadcast_to(0.5 * jnp.sum(part), out_ref.shape)


def choose_kernel(room, chip_ref, core_ref, *refs):
    part_refs, out_ref = refs[:-1], refs[-1]
    for place in range(room):
        core = core_ref[place]
        for k, part_ref in enumerate(part_refs):

            @pl.when(chip_ref[place] == k)
            def _(place=place, core=core, part_ref=part_ref):
                for level in range(out_ref.shape[0]):
                    out_ref[level, place] = part_ref[core, :, level]


def advance(total, weight, first, second):
    first = 0.9 * first + 0.1 * total
    second = 0.95 * second + 0.05 * total * total
    root = jnp.sqrt(second * (1.0 / (1.0 - 0.95**10))) + 1e-08
    step = (first * (1.0 / (1.0 - 0.9**10))) / root
    return weight - 0.1 * (step + 0.3 * weight), first, second


def update_kernel(slots, limit, *refs):
    source_ref, partner_ref, list_ref, count_ref, rank_ref, sum_ref, grad_ref = refs[:7]
    state_refs, out_ref = refs[7:-1], refs[-1]
    clip = jnp.minimum(jnp.float32(1.0), limit / jnp.sqrt(sum_ref[0:1, 0:1] + 1e-06))
    clip = jnp.broadcast_to(clip, (8, grad_ref.shape[3]))

    def gradient(slot, carry):
        source = source_ref[slot]
        other = partner_ref[source]
        for top in range(0, grad_ref.shape[2], 8):
            rows = pl.ds(top, 8)
            out_ref[slot, 0, rows] = clip * (
                grad_ref[source, 0, rows] + grad_ref[other, 0, rows]
            )
        return carry

    lax.fori_loop(0, slots, gradient, 0, unroll=4)

    def update(place, carry):
        slot = list_ref[place]
        source = source_ref[slot]
        rank = rank_ref[source]
        level = source // INNER
        start = 0
        for room, state_ref in zip(ROUNDS, state_refs):

            @pl.when((rank >= start) & (rank < start + room))
            def _(start=start, room=room, state_ref=state_ref):
                spot = jnp.clip(rank - start, 0, room - 1)
                for top in range(0, grad_ref.shape[2], 8):
                    rows = pl.ds(top, 8)
                    state = [grad_ref[source, 1, rows]]
                    state += [state_ref[level, spot, k, rows] for k in range(2)]
                    for k, value in enumerate(advance(out_ref[slot, 0, rows], *state)):
                        out_ref[slot, k, rows] = value

            start += room
        return carry

    lax.fori_loop(0, count_ref[0], update, 0)


def update(states, slots, limit, scalars, sumsq, spread):
    smem = pl.BlockSpec(memory_space=pltpu.SMEM)
    vmem = pl.BlockSpec(memory_space=pltpu.VMEM)
    return pl.pallas_call(
        functools.partial(update_kernel, slots, limit),
        out_shape=jax.ShapeDtypeStruct((slots, 3, *spread.shape[2:]), jnp.float32),
        in_specs=[smem] * len(scalars) + [vmem] * (2 + len(states)),
        out_specs=vmem,
        compiler_params=pltpu.CompilerParams(vmem_limit_bytes=16 * 2**20),
    )(*scalars, sumsq, spread, *states)


def finish_kernel(
    moved_ref, lane_ref, next_first, next_second, weight_ref, first_ref, second_ref, *outs
):
    @pl.when(moved_ref[0] != 0)
    def _():
        for lane, out in zip((lane_ref, next_first, next_second), outs):
            out[...] = lane[:, 0]

    @pl.when(moved_ref[0] == 0)
    def _():
        def one(piece, carry):
            for top in range(0, lane_ref.shape[2], 8):
                rows = pl.ds(top, 8)
                values = advance(
                    lane_ref[piece, 0, rows],
                    weight_ref[piece, rows],
                    first_ref[piece, rows],
                    second_ref[piece, rows],
                )
                for out, value in zip(outs, values):
                    out[piece, rows] = value
            return carry

        lax.fori_loop(0, lane_ref.shape[0], one, 0, unroll=4)


def finish(moved, lanes, blocks):
    slots, _, rows, hidden = lanes.shape
    group = slots // 4

    def lane(k):
        keep = (lambda i, moved: (i, 0, 0, 0)) if k == 0 else None
        index = keep or (lambda i, moved: (i * moved[0], k, 0, 0))
        return pl.BlockSpec((group, 1, rows, hidden), index)

    home = pl.BlockSpec((group, rows, hidden), lambda i, moved: (i * (1 - moved[0]), 0, 0))
    out = pl.BlockSpec((group, rows, hidden), lambda i, moved: (i, 0, 0))
    return pl.pallas_call(
        finish_kernel,
        grid_spec=pltpu.PrefetchScalarGridSpec(
            num_scalar_prefetch=1,
            grid=(slots // group,),
            in_specs=[lane(0), lane(1), lane(2), home, home, home],
            out_specs=[out] * 3,
        ),
        out_shape=[jax.ShapeDtypeStruct((slots, rows, hidden), jnp.float32)] * 3,
        compiler_params=pltpu.CompilerParams(vmem_limit_bytes=56 * 2**20),
    )(moved, lanes, lanes, lanes, *blocks)


def shifted(value, axis, pairs_of):
    total = value
    for pairs in pairs_of:
        total = total + lax.ppermute(value, axis, pairs)
    return total


def plane_sum(value, slots, inner):
    value = shifted(value, "expert", [[(i, i ^ 1) for i in range(slots)]])
    return shifted(
        value,
        "expert",
        [
            [(i, i // inner * inner + (i + k) % inner) for i in range(slots)]
            for k in range(2, inner, 2)
        ],
    )


def all_sum(value):
    slots = lax.axis_size("expert")
    width = lax.axis_size("mp")
    value = shifted(
        value, "mp", [[(i, (i + k) % width) for i in range(width)] for k in range(1, width)]
    )
    value = plane_sum(value, slots, INNER)
    half = slots // INNER // 2
    core = lax.axis_index("expert") % 2
    total = jnp.where(core == 0, value, jnp.zeros_like(value))
    for k in range(half):
        spots = [
            (i, (i + (k + i % 2 * half) * INNER) % slots) for i in range(slots) if k + i % 2
        ]
        total = total + lax.ppermute(value, "expert", spots)
    return shifted(total, "expert", [[(i, i ^ 1) for i in range(slots)]])


def pick(array, index, axis):
    return lax.dynamic_index_in_dim(array, index, axis, keepdims=False)


def within_plane(blocks, slots, rows):
    me = lax.axis_index("expert")
    chips = INNER // 2
    chip, core = me // 2 % chips, me % 2
    shape = (slots // INNER, chips, 2, rows, blocks[0].shape[-1])
    views = [block.reshape(shape) for block in blocks]
    other = jnp.stack([pick(view, 1 - core, 2) for view in views])
    mate = lax.ppermute(other, "expert", [(i, i ^ 1) for i in range(slots)])
    parts = []
    for k in range(chips):
        spot = (chip + k) % chips
        own = jnp.stack([pick(pick(view, spot, 1), core, 1) for view in views])
        part = jnp.stack([own, pick(mate, spot, 2)])
        if k:
            spots = [(i, i // INNER * INNER + (i + 2 * k) % INNER) for i in range(slots)]
            part = lax.ppermute(part, "expert", spots)
        parts.append(part)
    return tuple(parts)


def to_pieces(array):
    return lax.all_to_all(array, "expert", split_axis=0, concat_axis=0, tiled=True)


def along_planes(array, slots):
    groups = [[z * INNER + q for z in range(slots // INNER)] for q in range(INNER)]
    return lax.all_to_all(
        array, "expert", split_axis=0, concat_axis=0, tiled=True, axis_index_groups=groups
    )


def gather_states(room, place_slots, parts):
    me = lax.axis_index("expert")
    chip = (me // 2 - place_slots // 2) % (INNER // 2)
    core = (me + place_slots) % 2
    smem = pl.BlockSpec(memory_space=pltpu.SMEM)
    vmem = pl.BlockSpec(memory_space=pltpu.VMEM)
    _, lanes, levels, rows, hidden = parts[0].shape
    return pl.pallas_call(
        functools.partial(choose_kernel, room),
        out_shape=jax.ShapeDtypeStruct((levels, room, lanes, rows, hidden), jnp.float32),
        in_specs=[smem, smem] + [vmem] * len(parts),
        out_specs=vmem,
        compiler_params=pltpu.CompilerParams(vmem_limit_bytes=16 * 2**20),
    )(chip, core, *parts)


def on_device(
    tokens, cotangent, counts, place_now, partner, place_next, weight, first_moment, second_moment
):
    slots = lax.axis_size("expert")
    units = slots // 2
    width_dev = weight.shape[1]
    hidden = weight.shape[2]
    rows = width_dev // slots
    limit = 4.0 * math.sqrt(units * width_dev * lax.axis_size("mp") * hidden)

    pair = jnp.clip(partner, 0, slots - 1)
    equal = place_now[None, :] == place_next[:, None]
    lowest = jnp.argmax(equal, axis=1).astype(jnp.int32)
    source = jnp.where(place_now == place_next, jnp.arange(slots, dtype=jnp.int32), lowest)

    me = lax.axis_index("expert")
    moved = place_now != place_next
    slot_ids = jnp.arange(slots, dtype=jnp.int32)
    needed = jnp.any((source[None, :] == slot_ids[:, None]) & moved[None, :], axis=1)
    before = (slot_ids[None, :] < slot_ids[:, None]) & (
        slot_ids[None, :] // INNER == slot_ids[:, None] // INNER
    )
    rank = jnp.sum(jnp.where(before & needed[None, :], 1, 0), axis=1).astype(jnp.int32)
    most = jnp.max(jnp.where(needed, rank + 1, 0))
    mine = needed & (slot_ids // INNER == me // INNER)
    order = jnp.arange(INNER, dtype=jnp.int32)
    places = jnp.max(
        jnp.where(mine[None, :] & (rank[None, :] == order[:, None]), slot_ids[None, :], 0), axis=1
    ).astype(jnp.int32)

    moved_rank = jnp.sum(
        jnp.where((slot_ids[None, :] < slot_ids[:, None]) & moved[None, :], 1, 0), axis=1
    )
    moved_list = jnp.max(
        jnp.where(
            moved[None, :] & (moved_rank[None, :] == slot_ids[:, None]), slot_ids[None, :], 0
        ),
        axis=1,
    ).astype(jnp.int32)
    count = jnp.sum(jnp.where(moved, 1, 0)).astype(jnp.int32).reshape(1)

    parts = within_plane((first_moment[0], second_moment[0]), slots, rows)
    blocks = [
        array.reshape(slots, rows, hidden) for array in (weight, first_moment, second_moment)
    ]
    spread = to_pieces(grad_and_weight(tokens[0], cotangent[0], counts, blocks[0]))
    chosen = gather_states(ROUNDS[0], places[: ROUNDS[0]], parts)
    spread, chosen = lax.optimization_barrier((spread, chosen))
    states = along_planes(chosen, slots)

    smem = pl.BlockSpec(memory_space=pltpu.SMEM)
    part = pl.pallas_call(
        functools.partial(sumsq_kernel, slots),
        out_shape=jax.ShapeDtypeStruct((8, LANES), jnp.float32),
        in_specs=[smem, pl.BlockSpec(memory_space=pltpu.VMEM)],
        out_specs=pl.BlockSpec(memory_space=pltpu.VMEM),
        compiler_params=pltpu.CompilerParams(vmem_limit_bytes=8 * 2**20),
        cost_estimate=pl.CostEstimate(
            flops=spread.size, bytes_accessed=spread.size * 4, transcendentals=0
        ),
    )(pair, spread)
    sumsq = all_sum(part)

    scalars = (source, pair, moved_list, count, rank)

    def direct(states, parts, sumsq, spread):
        return update([states], slots, limit, scalars, sumsq, spread)

    def with_rest(states, parts, sumsq, spread):
        rest = along_planes(gather_states(ROUNDS[1], places[ROUNDS[0] :], parts), slots)
        return update([states, rest], slots, limit, scalars, sumsq, spread)

    out = lax.cond(most > ROUNDS[0], with_rest, direct, states, parts, sumsq, spread)
    out = to_pieces(out)
    mine = pick(moved, me, 0).astype(jnp.int32).reshape(1)
    parts = finish(mine, out, blocks)
    return tuple(part.reshape(weight.shape) for part in parts)


def solution(mesh):
    placed = (
        P("expert", None, "mp"),
        P("expert", None, None),
        P("expert"),
        P(),
        P(),
        P(),
        P("expert", "mp", None),
        P("expert", "mp", None),
        P("expert", "mp", None),
    )
    return jax.shard_map(
        on_device,
        mesh=mesh,
        in_specs=placed,
        out_specs=(P("expert", "mp", None), P("expert", "mp", None), P("expert", "mp", None)),
        check_vma=False,
    )
```

```python
import functools
import math

import jax
import jax.numpy as jnp
from jax import lax
from jax.experimental import pallas as pl
from jax.experimental.pallas import tpu as pltpu
from jax.sharding import PartitionSpec as P

LANES = 128
INNER = 8
ROOM = 4
MORE = (1, 2, 4)


def grad_kernel(live_ref, block_ref, rows_ref, weight_ref, out_ref):
    rows = rows_ref[...].astype(jnp.float32)
    row_ids = lax.broadcasted_iota(jnp.int32, rows.shape, 0)
    masked = jnp.where(row_ids < live_ref[0], rows, jnp.zeros_like(rows)).astype(jnp.bfloat16)
    grads = lax.dot_general(
        block_ref[...], masked, (((0,), (0,)), ((), ())), preferred_element_type=jnp.float32
    )
    out_ref[:, 0] = grads.reshape(weight_ref.shape)
    out_ref[:, 1] = weight_ref[...]


def grad_and_weight(block, grad_rows, live, weight):
    rows, width = block.shape
    pieces, piece_rows, hidden = weight.shape
    steps = 2
    tile, group = width // steps, pieces // steps
    return pl.pallas_call(
        grad_kernel,
        grid=(steps,),
        out_shape=jax.ShapeDtypeStruct((pieces, 2, piece_rows, hidden), jnp.float32),
        in_specs=[
            pl.BlockSpec(memory_space=pltpu.SMEM),
            pl.BlockSpec((rows, tile), lambda i: (0, i)),
            pl.BlockSpec((rows, hidden), lambda i: (0, 0)),
            pl.BlockSpec((group, piece_rows, hidden), lambda i: (i, 0, 0)),
        ],
        out_specs=pl.BlockSpec((group, 2, piece_rows, hidden), lambda i: (i, 0, 0, 0)),
        compiler_params=pltpu.CompilerParams(vmem_limit_bytes=56 * 2**20),
        cost_estimate=pl.CostEstimate(
            flops=2 * rows * width * hidden,
            bytes_accessed=2 * rows * (width + hidden) + 12 * width * hidden,
            transcendentals=0,
        ),
    )(live, block, grad_rows, weight)


def sumsq_kernel(slots, partner_ref, grad_ref, out_ref):
    def body(slot, acc):
        raw = grad_ref[slot, 0] + grad_ref[partner_ref[slot], 0]
        return acc + raw * raw

    zero = jnp.zeros(grad_ref.shape[2:], jnp.float32)
    acc = lax.fori_loop(0, slots, body, zero, unroll=4)
    rows, cols = acc.shape
    part = sum(
        acc[r : r + 8, c : c + LANES] for r in range(0, rows, 8) for c in range(0, cols, LANES)
    )
    out_ref[...] = jnp.broadcast_to(0.5 * jnp.sum(part), out_ref.shape)


def choose_kernel(room, chip_ref, core_ref, *refs):
    part_refs, out_ref = refs[:-1], refs[-1]
    for place in range(room):
        core = core_ref[place]
        for k, part_ref in enumerate(part_refs):

            @pl.when(chip_ref[place] == k)
            def _(place=place, core=core, part_ref=part_ref):
                for level in range(out_ref.shape[0]):
                    out_ref[level, place] = part_ref[core, :, level]


def advance(total, weight, first, second):
    first = 0.9 * first + 0.1 * total
    second = 0.95 * second + 0.05 * total * total
    root = jnp.sqrt(second * (1.0 / (1.0 - 0.95**10))) + 1e-08
    step = (first * (1.0 / (1.0 - 0.9**10))) / root
    return weight - 0.1 * (step + 0.3 * weight), first, second


def update_kernel(slots, limit, rooms, *refs):
    source_ref, partner_ref, list_ref, count_ref, rank_ref, sum_ref, grad_ref = refs[:7]
    state_refs, out_ref = refs[7:-1], refs[-1]
    clip = jnp.minimum(jnp.float32(1.0), limit / jnp.sqrt(sum_ref[0:1, 0:1] + 1e-06))
    clip = jnp.broadcast_to(clip, (8, grad_ref.shape[3]))

    def gradient(slot, carry):
        source = source_ref[slot]
        other = partner_ref[source]
        for top in range(0, grad_ref.shape[2], 8):
            rows = pl.ds(top, 8)
            out_ref[slot, 0, rows] = clip * (
                grad_ref[source, 0, rows] + grad_ref[other, 0, rows]
            )
        return carry

    lax.fori_loop(0, slots, gradient, 0, unroll=8)

    def update(place, carry):
        slot = list_ref[place]
        source = source_ref[slot]
        rank = rank_ref[source]
        level = source // INNER
        start = 0
        for room, state_ref in zip(rooms, state_refs):

            @pl.when((rank >= start) & (rank < start + room))
            def _(start=start, room=room, state_ref=state_ref):
                spot = jnp.clip(rank - start, 0, room - 1)
                for top in range(0, grad_ref.shape[2], 8):
                    rows = pl.ds(top, 8)
                    state = [grad_ref[source, 1, rows]]
                    state += [state_ref[level, spot, k, rows] for k in range(2)]
                    for k, value in enumerate(advance(out_ref[slot, 0, rows], *state)):
                        out_ref[slot, k, rows] = value

            start += room
        return carry

    lax.fori_loop(0, count_ref[0], update, 0)


def update(states, slots, limit, scalars, sumsq, spread):
    smem = pl.BlockSpec(memory_space=pltpu.SMEM)
    vmem = pl.BlockSpec(memory_space=pltpu.VMEM)
    return pl.pallas_call(
        functools.partial(update_kernel, slots, limit, [state.shape[1] for state in states]),
        out_shape=jax.ShapeDtypeStruct((slots, 3, *spread.shape[2:]), jnp.float32),
        in_specs=[smem] * len(scalars) + [vmem] * (2 + len(states)),
        out_specs=vmem,
        compiler_params=pltpu.CompilerParams(vmem_limit_bytes=16 * 2**20),
    )(*scalars, sumsq, spread, *states)


def finish_kernel(
    moved_ref, lane_ref, next_first, next_second, weight_ref, first_ref, second_ref, *outs
):
    @pl.when(moved_ref[0] != 0)
    def _():
        for lane, out in zip((lane_ref, next_first, next_second), outs):
            out[...] = lane[:, 0]

    @pl.when(moved_ref[0] == 0)
    def _():
        def one(piece, carry):
            for top in range(0, lane_ref.shape[2], 8):
                rows = pl.ds(top, 8)
                values = advance(
                    lane_ref[piece, 0, rows],
                    weight_ref[piece, rows],
                    first_ref[piece, rows],
                    second_ref[piece, rows],
                )
                for out, value in zip(outs, values):
                    out[piece, rows] = value
            return carry

        lax.fori_loop(0, lane_ref.shape[0], one, 0, unroll=4)


def finish(moved, lanes, blocks):
    slots, _, rows, hidden = lanes.shape
    group = slots // 4

    def lane(k):
        keep = (lambda i, moved: (i, 0, 0, 0)) if k == 0 else None
        index = keep or (lambda i, moved: (i * moved[0], k, 0, 0))
        return pl.BlockSpec((group, 1, rows, hidden), index)

    home = pl.BlockSpec((group, rows, hidden), lambda i, moved: (i * (1 - moved[0]), 0, 0))
    out = pl.BlockSpec((group, rows, hidden), lambda i, moved: (i, 0, 0))
    return pl.pallas_call(
        finish_kernel,
        grid_spec=pltpu.PrefetchScalarGridSpec(
            num_scalar_prefetch=1,
            grid=(slots // group,),
            in_specs=[lane(0), lane(1), lane(2), home, home, home],
            out_specs=[out] * 3,
        ),
        out_shape=[jax.ShapeDtypeStruct((slots, rows, hidden), jnp.float32)] * 3,
        compiler_params=pltpu.CompilerParams(vmem_limit_bytes=56 * 2**20),
    )(moved, lanes, lanes, lanes, *blocks)


def shifted(value, axis, pairs_of):
    total = value
    for pairs in pairs_of:
        total = total + lax.ppermute(value, axis, pairs)
    return total


def plane_sum(value, slots, inner):
    value = shifted(value, "expert", [[(i, i ^ 1) for i in range(slots)]])
    return shifted(
        value,
        "expert",
        [
            [(i, i // inner * inner + (i + k) % inner) for i in range(slots)]
            for k in range(2, inner, 2)
        ],
    )


def all_sum(value):
    slots = lax.axis_size("expert")
    width = lax.axis_size("mp")
    value = shifted(
        value, "mp", [[(i, (i + k) % width) for i in range(width)] for k in range(1, width)]
    )
    value = plane_sum(value, slots, INNER)
    half = slots // INNER // 2
    core = lax.axis_index("expert") % 2
    total = jnp.where(core == 0, value, jnp.zeros_like(value))
    for k in range(half):
        spots = [
            (i, (i + (k + i % 2 * half) * INNER) % slots) for i in range(slots) if k + i % 2
        ]
        total = total + lax.ppermute(value, "expert", spots)
    return shifted(total, "expert", [[(i, i ^ 1) for i in range(slots)]])


def pick(array, index, axis):
    return lax.dynamic_index_in_dim(array, index, axis, keepdims=False)


def within_plane(blocks, slots, rows):
    me = lax.axis_index("expert")
    chips = INNER // 2
    chip, core = me // 2 % chips, me % 2
    shape = (slots // INNER, chips, 2, rows, blocks[0].shape[-1])
    views = [block.reshape(shape) for block in blocks]
    other = jnp.stack([pick(view, 1 - core, 2) for view in views])
    mate = lax.ppermute(other, "expert", [(i, i ^ 1) for i in range(slots)])
    parts = []
    for k in range(chips):
        spot = (chip + k) % chips
        own = jnp.stack([pick(pick(view, spot, 1), core, 1) for view in views])
        part = jnp.stack([own, pick(mate, spot, 2)])
        if k:
            spots = [(i, i // INNER * INNER + (i + 2 * k) % INNER) for i in range(slots)]
            part = lax.ppermute(part, "expert", spots)
        parts.append(part)
    return tuple(parts)


def to_pieces(array):
    return lax.all_to_all(array, "expert", split_axis=0, concat_axis=0, tiled=True)


def along_planes(array, slots):
    groups = [[z * INNER + q for z in range(slots // INNER)] for q in range(INNER)]
    return lax.all_to_all(
        array, "expert", split_axis=0, concat_axis=0, tiled=True, axis_index_groups=groups
    )


def gather_states(room, place_slots, parts):
    me = lax.axis_index("expert")
    chip = (me // 2 - place_slots // 2) % (INNER // 2)
    core = (me + place_slots) % 2
    smem = pl.BlockSpec(memory_space=pltpu.SMEM)
    vmem = pl.BlockSpec(memory_space=pltpu.VMEM)
    _, lanes, levels, rows, hidden = parts[0].shape
    return pl.pallas_call(
        functools.partial(choose_kernel, room),
        out_shape=jax.ShapeDtypeStruct((levels, room, lanes, rows, hidden), jnp.float32),
        in_specs=[smem, smem] + [vmem] * len(parts),
        out_specs=vmem,
        compiler_params=pltpu.CompilerParams(vmem_limit_bytes=16 * 2**20),
    )(chip, core, *parts)


def on_device(
    tokens, cotangent, counts, place_now, partner, place_next, weight, first_moment, second_moment
):
    slots = lax.axis_size("expert")
    units = slots // 2
    width_dev = weight.shape[1]
    hidden = weight.shape[2]
    rows = width_dev // slots
    limit = 4.0 * math.sqrt(units * width_dev * lax.axis_size("mp") * hidden)

    pair = jnp.clip(partner, 0, slots - 1)
    equal = place_now[None, :] == place_next[:, None]
    lowest = jnp.argmax(equal, axis=1).astype(jnp.int32)
    source = jnp.where(place_now == place_next, jnp.arange(slots, dtype=jnp.int32), lowest)

    me = lax.axis_index("expert")
    moved = place_now != place_next
    slot_ids = jnp.arange(slots, dtype=jnp.int32)
    needed = jnp.any((source[None, :] == slot_ids[:, None]) & moved[None, :], axis=1)
    before = (slot_ids[None, :] < slot_ids[:, None]) & (
        slot_ids[None, :] // INNER == slot_ids[:, None] // INNER
    )
    rank = jnp.sum(jnp.where(before & needed[None, :], 1, 0), axis=1).astype(jnp.int32)
    most = jnp.max(jnp.where(needed, rank + 1, 0))
    mine = needed & (slot_ids // INNER == me // INNER)
    order = jnp.arange(INNER, dtype=jnp.int32)
    places = jnp.max(
        jnp.where(mine[None, :] & (rank[None, :] == order[:, None]), slot_ids[None, :], 0), axis=1
    ).astype(jnp.int32)

    moved_rank = jnp.sum(
        jnp.where((slot_ids[None, :] < slot_ids[:, None]) & moved[None, :], 1, 0), axis=1
    )
    moved_list = jnp.max(
        jnp.where(
            moved[None, :] & (moved_rank[None, :] == slot_ids[:, None]), slot_ids[None, :], 0
        ),
        axis=1,
    ).astype(jnp.int32)
    count = jnp.sum(jnp.where(moved, 1, 0)).astype(jnp.int32).reshape(1)

    parts = within_plane((first_moment[0], second_moment[0]), slots, rows)
    blocks = [
        array.reshape(slots, rows, hidden) for array in (weight, first_moment, second_moment)
    ]
    spread = to_pieces(grad_and_weight(tokens[0], cotangent[0], counts, blocks[0]))
    chosen = gather_states(ROOM, places[:ROOM], parts)
    spread, chosen = lax.optimization_barrier((spread, chosen))
    states = along_planes(chosen, slots)

    smem = pl.BlockSpec(memory_space=pltpu.SMEM)
    part = pl.pallas_call(
        functools.partial(sumsq_kernel, slots),
        out_shape=jax.ShapeDtypeStruct((8, LANES), jnp.float32),
        in_specs=[smem, pl.BlockSpec(memory_space=pltpu.VMEM)],
        out_specs=pl.BlockSpec(memory_space=pltpu.VMEM),
        compiler_params=pltpu.CompilerParams(vmem_limit_bytes=8 * 2**20),
        cost_estimate=pl.CostEstimate(
            flops=spread.size, bytes_accessed=spread.size * 4, transcendentals=0
        ),
    )(pair, spread)
    sumsq = all_sum(part)

    scalars = (source, pair, moved_list, count, rank)

    def direct(states, parts, sumsq, spread):
        return update([states], slots, limit, scalars, sumsq, spread)

    def with_more(room, states, parts, sumsq, spread):
        more = along_planes(gather_states(room, places[ROOM : ROOM + room], parts), slots)
        return update([states, more], slots, limit, scalars, sumsq, spread)

    branches = [direct] + [functools.partial(with_more, room) for room in MORE]
    branch = sum((most > ROOM + room).astype(jnp.int32) for room in (0, *MORE[:-1]))
    out = lax.switch(branch, branches, states, parts, sumsq, spread)
    out = to_pieces(out)
    mine = pick(moved, me, 0).astype(jnp.int32).reshape(1)
    parts = finish(mine, out, blocks)
    return tuple(part.reshape(weight.shape) for part in parts)


def solution(mesh):
    placed = (
        P("expert", None, "mp"),
        P("expert", None, None),
        P("expert"),
        P(),
        P(),
        P(),
        P("expert", "mp", None),
        P("expert", "mp", None),
        P("expert", "mp", None),
    )
    return jax.shard_map(
        on_device,
        mesh=mesh,
        in_specs=placed,
        out_specs=(P("expert", "mp", None), P("expert", "mp", None), P("expert", "mp", None)),
        check_vma=False,
    )
```

```python
import functools
import math

import jax
import jax.numpy as jnp
from jax import lax
from jax.experimental import pallas as pl
from jax.experimental.pallas import tpu as pltpu
from jax.sharding import PartitionSpec as P

LANES = 128
INNER = 8
ROOM = 4
MORE = (1, 2, 4)


def grad_kernel(live_ref, block_ref, rows_ref, weight_ref, out_ref):
    rows = rows_ref[...].astype(jnp.float32)
    row_ids = lax.broadcasted_iota(jnp.int32, rows.shape, 0)
    masked = jnp.where(row_ids < live_ref[0], rows, jnp.zeros_like(rows)).astype(jnp.bfloat16)
    grads = lax.dot_general(
        block_ref[...], masked, (((0,), (0,)), ((), ())), preferred_element_type=jnp.float32
    )
    out_ref[:, 0] = grads.reshape(weight_ref.shape)
    out_ref[:, 1] = weight_ref[...]


def grad_and_weight(block, grad_rows, live, weight):
    rows, width = block.shape
    pieces, piece_rows, hidden = weight.shape
    steps = 2
    tile, group = width // steps, pieces // steps
    return pl.pallas_call(
        grad_kernel,
        grid=(steps,),
        out_shape=jax.ShapeDtypeStruct((pieces, 2, piece_rows, hidden), jnp.float32),
        in_specs=[
            pl.BlockSpec(memory_space=pltpu.SMEM),
            pl.BlockSpec((rows, tile), lambda i: (0, i)),
            pl.BlockSpec((rows, hidden), lambda i: (0, 0)),
            pl.BlockSpec((group, piece_rows, hidden), lambda i: (i, 0, 0)),
        ],
        out_specs=pl.BlockSpec((group, 2, piece_rows, hidden), lambda i: (i, 0, 0, 0)),
        compiler_params=pltpu.CompilerParams(vmem_limit_bytes=56 * 2**20),
        cost_estimate=pl.CostEstimate(
            flops=2 * rows * width * hidden,
            bytes_accessed=2 * rows * (width + hidden) + 12 * width * hidden,
            transcendentals=0,
        ),
    )(live, block, grad_rows, weight)


def sumsq_kernel(slots, partner_ref, grad_ref, out_ref):
    def body(slot, acc):
        raw = grad_ref[slot, 0] + grad_ref[partner_ref[slot], 0]
        return acc + raw * raw

    zero = jnp.zeros(grad_ref.shape[2:], jnp.float32)
    acc = lax.fori_loop(0, slots, body, zero, unroll=4)
    rows, cols = acc.shape
    part = sum(
        acc[r : r + 8, c : c + LANES] for r in range(0, rows, 8) for c in range(0, cols, LANES)
    )
    out_ref[...] = jnp.broadcast_to(0.5 * jnp.sum(part), out_ref.shape)


def choose_kernel(room, chip_ref, core_ref, *refs):
    part_refs, out_ref = refs[:-1], refs[-1]
    for place in range(room):
        core = core_ref[place]
        for k, part_ref in enumerate(part_refs):

            @pl.when(chip_ref[place] == k)
            def _(place=place, core=core, part_ref=part_ref):
                for level in range(out_ref.shape[0]):
                    out_ref[level, place] = part_ref[core, :, level]


def advance(total, weight, first, second):
    first = 0.9 * first + 0.1 * total
    second = 0.95 * second + 0.05 * total * total
    root = jnp.sqrt(second * (1.0 / (1.0 - 0.95**10))) + 1e-08
    step = (first * (1.0 / (1.0 - 0.9**10))) / root
    return weight - 0.1 * (step + 0.3 * weight), first, second


def update_kernel(slots, limit, rooms, *refs):
    source_ref, partner_ref, list_ref, count_ref, rank_ref, sum_ref, grad_ref = refs[:7]
    state_refs, out_ref = refs[7:-1], refs[-1]
    clip = jnp.minimum(jnp.float32(1.0), limit / jnp.sqrt(sum_ref[0:1, 0:1] + 1e-06))
    clip = jnp.broadcast_to(clip, (8, grad_ref.shape[3]))

    def gradient(slot, carry):
        source = source_ref[slot]
        other = partner_ref[source]
        for top in range(0, grad_ref.shape[2], 8):
            rows = pl.ds(top, 8)
            out_ref[slot, 0, rows] = clip * (
                grad_ref[source, 0, rows] + grad_ref[other, 0, rows]
            )
        return carry

    lax.fori_loop(0, slots, gradient, 0, unroll=8)

    def update(place, carry):
        slot = list_ref[place]
        source = source_ref[slot]
        rank = rank_ref[source]
        level = source // INNER
        start = 0
        for room, state_ref in zip(rooms, state_refs):

            def advance_slot(start=start, room=room, state_ref=state_ref):
                spot = jnp.clip(rank - start, 0, room - 1)
                state = [grad_ref[source, 1]] + [state_ref[level, spot, k] for k in range(2)]
                for k, value in enumerate(advance(out_ref[slot, 0], *state)):
                    out_ref[slot, k] = value

            if len(rooms) == 1:
                advance_slot()
            else:
                pl.when((rank >= start) & (rank < start + room))(advance_slot)

            start += room
        return carry

    lax.fori_loop(0, count_ref[0], update, 0)


def update(states, slots, limit, scalars, sumsq, spread):
    smem = pl.BlockSpec(memory_space=pltpu.SMEM)
    vmem = pl.BlockSpec(memory_space=pltpu.VMEM)
    return pl.pallas_call(
        functools.partial(update_kernel, slots, limit, [state.shape[1] for state in states]),
        out_shape=jax.ShapeDtypeStruct((slots, 3, *spread.shape[2:]), jnp.float32),
        in_specs=[smem] * len(scalars) + [vmem] * (2 + len(states)),
        out_specs=vmem,
        compiler_params=pltpu.CompilerParams(vmem_limit_bytes=16 * 2**20),
    )(*scalars, sumsq, spread, *states)


def finish_kernel(
    moved_ref, lane_ref, next_first, next_second, weight_ref, first_ref, second_ref, *outs
):
    @pl.when(moved_ref[0] != 0)
    def _():
        for lane, out in zip((lane_ref, next_first, next_second), outs):
            out[...] = lane[:, 0]

    @pl.when(moved_ref[0] == 0)
    def _():
        def one(piece, carry):
            for top in range(0, lane_ref.shape[2], 8):
                rows = pl.ds(top, 8)
                values = advance(
                    lane_ref[piece, 0, rows],
                    weight_ref[piece, rows],
                    first_ref[piece, rows],
                    second_ref[piece, rows],
                )
                for out, value in zip(outs, values):
                    out[piece, rows] = value
            return carry

        lax.fori_loop(0, lane_ref.shape[0], one, 0, unroll=4)


def finish(moved, lanes, blocks):
    slots, _, rows, hidden = lanes.shape
    group = slots // 4

    def lane(k):
        keep = (lambda i, moved: (i, 0, 0, 0)) if k == 0 else None
        index = keep or (lambda i, moved: (i * moved[0], k, 0, 0))
        return pl.BlockSpec((group, 1, rows, hidden), index)

    home = pl.BlockSpec((group, rows, hidden), lambda i, moved: (i * (1 - moved[0]), 0, 0))
    out = pl.BlockSpec((group, rows, hidden), lambda i, moved: (i, 0, 0))
    return pl.pallas_call(
        finish_kernel,
        grid_spec=pltpu.PrefetchScalarGridSpec(
            num_scalar_prefetch=1,
            grid=(slots // group,),
            in_specs=[lane(0), lane(1), lane(2), home, home, home],
            out_specs=[out] * 3,
        ),
        out_shape=[jax.ShapeDtypeStruct((slots, rows, hidden), jnp.float32)] * 3,
        compiler_params=pltpu.CompilerParams(vmem_limit_bytes=56 * 2**20),
    )(moved, lanes, lanes, lanes, *blocks)


def shifted(value, axis, pairs_of):
    total = value
    for pairs in pairs_of:
        total = total + lax.ppermute(value, axis, pairs)
    return total


def plane_sum(value, slots, inner):
    value = shifted(value, "expert", [[(i, i ^ 1) for i in range(slots)]])
    return shifted(
        value,
        "expert",
        [
            [(i, i // inner * inner + (i + k) % inner) for i in range(slots)]
            for k in range(2, inner, 2)
        ],
    )


def all_sum(value):
    slots = lax.axis_size("expert")
    width = lax.axis_size("mp")
    value = shifted(
        value, "mp", [[(i, (i + k) % width) for i in range(width)] for k in range(1, width)]
    )
    value = plane_sum(value, slots, INNER)
    half = slots // INNER // 2
    core = lax.axis_index("expert") % 2
    total = jnp.where(core == 0, value, jnp.zeros_like(value))
    for k in range(half):
        spots = [
            (i, (i + (k + i % 2 * half) * INNER) % slots) for i in range(slots) if k + i % 2
        ]
        total = total + lax.ppermute(value, "expert", spots)
    return shifted(total, "expert", [[(i, i ^ 1) for i in range(slots)]])


def pick(array, index, axis):
    return lax.dynamic_index_in_dim(array, index, axis, keepdims=False)


def within_plane(blocks, slots, rows):
    me = lax.axis_index("expert")
    chips = INNER // 2
    chip, core = me // 2 % chips, me % 2
    shape = (slots // INNER, chips, 2, rows, blocks[0].shape[-1])
    views = [block.reshape(shape) for block in blocks]
    other = jnp.stack([pick(view, 1 - core, 2) for view in views])
    mate = lax.ppermute(other, "expert", [(i, i ^ 1) for i in range(slots)])
    parts = []
    for k in range(chips):
        spot = (chip + k) % chips
        own = jnp.stack([pick(pick(view, spot, 1), core, 1) for view in views])
        part = jnp.stack([own, pick(mate, spot, 2)])
        if k:
            spots = [(i, i // INNER * INNER + (i + 2 * k) % INNER) for i in range(slots)]
            part = lax.ppermute(part, "expert", spots)
        parts.append(part)
    return tuple(parts)


def to_pieces(array):
    return lax.all_to_all(array, "expert", split_axis=0, concat_axis=0, tiled=True)


def along_planes(array, slots):
    groups = [[z * INNER + q for z in range(slots // INNER)] for q in range(INNER)]
    return lax.all_to_all(
        array, "expert", split_axis=0, concat_axis=0, tiled=True, axis_index_groups=groups
    )


def gather_states(room, place_slots, parts):
    me = lax.axis_index("expert")
    chip = (me // 2 - place_slots // 2) % (INNER // 2)
    core = (me + place_slots) % 2
    smem = pl.BlockSpec(memory_space=pltpu.SMEM)
    vmem = pl.BlockSpec(memory_space=pltpu.VMEM)
    _, lanes, levels, rows, hidden = parts[0].shape
    return pl.pallas_call(
        functools.partial(choose_kernel, room),
        out_shape=jax.ShapeDtypeStruct((levels, room, lanes, rows, hidden), jnp.float32),
        in_specs=[smem, smem] + [vmem] * len(parts),
        out_specs=vmem,
        compiler_params=pltpu.CompilerParams(vmem_limit_bytes=16 * 2**20),
    )(chip, core, *parts)


def on_device(
    tokens, cotangent, counts, place_now, partner, place_next, weight, first_moment, second_moment
):
    slots = lax.axis_size("expert")
    units = slots // 2
    width_dev = weight.shape[1]
    hidden = weight.shape[2]
    rows = width_dev // slots
    limit = 4.0 * math.sqrt(units * width_dev * lax.axis_size("mp") * hidden)

    pair = jnp.clip(partner, 0, slots - 1)
    equal = place_now[None, :] == place_next[:, None]
    lowest = jnp.argmax(equal, axis=1).astype(jnp.int32)
    source = jnp.where(place_now == place_next, jnp.arange(slots, dtype=jnp.int32), lowest)

    me = lax.axis_index("expert")
    moved = place_now != place_next
    slot_ids = jnp.arange(slots, dtype=jnp.int32)
    needed = jnp.any((source[None, :] == slot_ids[:, None]) & moved[None, :], axis=1)
    before = (slot_ids[None, :] < slot_ids[:, None]) & (
        slot_ids[None, :] // INNER == slot_ids[:, None] // INNER
    )
    rank = jnp.sum(jnp.where(before & needed[None, :], 1, 0), axis=1).astype(jnp.int32)
    most = jnp.max(jnp.where(needed, rank + 1, 0))
    mine = needed & (slot_ids // INNER == me // INNER)
    order = jnp.arange(INNER, dtype=jnp.int32)
    places = jnp.max(
        jnp.where(mine[None, :] & (rank[None, :] == order[:, None]), slot_ids[None, :], 0), axis=1
    ).astype(jnp.int32)

    moved_rank = jnp.sum(
        jnp.where((slot_ids[None, :] < slot_ids[:, None]) & moved[None, :], 1, 0), axis=1
    )
    moved_list = jnp.max(
        jnp.where(
            moved[None, :] & (moved_rank[None, :] == slot_ids[:, None]), slot_ids[None, :], 0
        ),
        axis=1,
    ).astype(jnp.int32)
    count = jnp.sum(jnp.where(moved, 1, 0)).astype(jnp.int32).reshape(1)

    parts = within_plane((first_moment[0], second_moment[0]), slots, rows)
    blocks = [
        array.reshape(slots, rows, hidden) for array in (weight, first_moment, second_moment)
    ]
    spread = to_pieces(grad_and_weight(tokens[0], cotangent[0], counts, blocks[0]))
    chosen = gather_states(ROOM, places[:ROOM], parts)
    scalars = (source, pair, moved_list, count, rank)
    branch = sum((most > ROOM + room).astype(jnp.int32) for room in (0, *MORE[:-1]))
    chosen, scalars, branch = lax.optimization_barrier((chosen, scalars, branch))
    spread, chosen = lax.optimization_barrier((spread, chosen))
    states = along_planes(chosen, slots)

    smem = pl.BlockSpec(memory_space=pltpu.SMEM)
    part = pl.pallas_call(
        functools.partial(sumsq_kernel, slots),
        out_shape=jax.ShapeDtypeStruct((8, LANES), jnp.float32),
        in_specs=[smem, pl.BlockSpec(memory_space=pltpu.VMEM)],
        out_specs=pl.BlockSpec(memory_space=pltpu.VMEM),
        compiler_params=pltpu.CompilerParams(vmem_limit_bytes=8 * 2**20),
        cost_estimate=pl.CostEstimate(
            flops=spread.size, bytes_accessed=spread.size * 4, transcendentals=0
        ),
    )(pair, spread)
    sumsq = all_sum(part)


    def direct(states, parts, sumsq, spread):
        return update([states], slots, limit, scalars, sumsq, spread)

    def with_more(room, states, parts, sumsq, spread):
        more = along_planes(gather_states(room, places[ROOM : ROOM + room], parts), slots)
        return update([states, more], slots, limit, scalars, sumsq, spread)

    branches = [direct] + [functools.partial(with_more, room) for room in MORE]
    out = lax.switch(branch, branches, states, parts, sumsq, spread)
    out = to_pieces(out)
    mine = pick(moved, me, 0).astype(jnp.int32).reshape(1)
    parts = finish(mine, out, blocks)
    return tuple(part.reshape(weight.shape) for part in parts)


def solution(mesh):
    placed = (
        P("expert", None, "mp"),
        P("expert", None, None),
        P("expert"),
        P(),
        P(),
        P(),
        P("expert", "mp", None),
        P("expert", "mp", None),
        P("expert", "mp", None),
    )
    return jax.shard_map(
        on_device,
        mesh=mesh,
        in_specs=placed,
        out_specs=(P("expert", "mp", None), P("expert", "mp", None), P("expert", "mp", None)),
        check_vma=False,
    )
```
